256 devices in a mesh: dp: 8 (over y, core), mp: 32 (over x, z).
Axes of the slice: x: 4, y: 4, z: 8, core: 2. Of those that a mesh axis runs over, the one named last changes fastest.
Arguments:
- acts_in: bfloat16 [65536, 4096], P(('dp', 'mp')), may hold values from -6 to 6
- grad_in: bfloat16 [65536, 8192], P('dp', 'mp'), may hold values from -0.0234375 to 0.0234375
- acts_out: bfloat16 [65536, 8192], P('dp', 'mp'), may hold values from -6 to 6
- grad_out: bfloat16 [65536, 4096], P(('dp', 'mp')), may hold values from -0.0234375 to 0.0234375
- basis_in: bfloat16 [4096, 256], P('mp'), may hold values from -0.09375 to 0.09375
- basis_out: bfloat16 [4096, 256], P('mp'), may hold values from -0.09375 to 0.09375
- first_in: float32 [256, 8192], P('dp', 'mp'), may hold values from -1.8 to 1.8
- second_in: float32 [256, 8192], P('dp', 'mp'), may hold values from 0.0001 to 0.01
- first_out: float32 [256, 8192], P('dp', 'mp'), may hold values from -1.8 to 1.8
- second_out: float32 [256, 8192], P('dp', 'mp'), may hold values from 0.0001 to 0.01
Outputs:
- delta_in: bfloat16 [4096, 8192], P(None, 'mp')
- delta_out: bfloat16 [8192, 4096], P('mp')
- new_first_in: float32 [256, 8192], P('dp', 'mp')
- new_second_in: float32 [256, 8192], P('dp', 'mp')
- new_first_out: float32 [256, 8192], P('dp', 'mp')
- new_second_out: float32 [256, 8192], P('dp', 'mp')
The draws below stay inside these ranges and needn't reach their ends.
All inputs are finite; a program needn't handle non-finite values.
Results may differ from the reference program's by a relative error of at most 0.0058.
Values may be sent and summed in bfloat16 or wider, within the bound.
No kernel may reach another device: no remote copies, remote signals or barrier semaphores. Data moves between devices by JAX's collectives and lax.ppermute only.
A program may use at most 128 MiB of HBM per device.

```python
import math
import jax
import jax.numpy as jnp
from jax import lax

D = 4096
INNER = 8192
R = 256
TOK_DEV = 256
TOKENS = 65536
N_DP = 8
N_MP = 32


def block_scale(own_key, dims, cuts, smallest, largest):
    level, own = 1.0, jax.random.fold_in(own_key, 6)
    for position, shards_of in cuts:
        draws = jnp.exp(jax.random.uniform(jax.random.fold_in(own, position), (shards_of,), jnp.float32, smallest / len(cuts), largest / len(cuts)))
        level = level * jnp.repeat(draws, dims[position] // shards_of).reshape([-1 if axis == position else 1 for axis in range(len(dims))])
    return level


def normal_values(rng, shape, scale, bound, cuts=(), dtype=jnp.bfloat16):
    result = scale * jax.random.normal(rng, shape, jnp.float32)
    if cuts:
        result = result * block_scale(rng, shape, cuts, -0.22, 0.18)
    return jnp.clip(result, -bound, bound).astype(dtype)


def setup_inputs(seed: int = 0) -> dict:
    seeds = jax.random.split(jax.random.key(seed), 11)
    acts_in = normal_values(seeds[0], (TOKENS, D), 1.0, 6.0, ((0, 256),))
    grad_in = normal_values(seeds[1], (TOKENS, INNER), ((TOK_DEV * N_MP * N_DP) ** -0.5), 0.0234375, ((0, 8), (1, 32)))
    acts_out = normal_values(seeds[2], (TOKENS, INNER), 1.0, 6.0, ((0, 8), (1, 32)))
    grad_out = normal_values(seeds[3], (TOKENS, D), ((TOK_DEV * N_MP * N_DP) ** -0.5), 0.0234375, ((0, 256),))
    basis_in = normal_values(seeds[4], (D, R), D ** -0.5, 0.09375, ((0, 32),))
    basis_out = normal_values(seeds[5], (D, R), D ** -0.5, 0.09375, ((0, 32),))
    first_in = normal_values(seeds[6], (R, INNER), 0.3, 1.8, ((0, 8), (1, 32)), jnp.float32)
    second_in = jnp.clip(jnp.exp(math.log(0.01) - 4.6051702 * jax.random.uniform(seeds[7], (R, INNER), jnp.float32) ** block_scale(seeds[7], (R, INNER), ((0, 8), (1, 32)), -0.2, 0.2)), 0.0001, 0.01)
    first_out = normal_values(seeds[8], (R, INNER), 0.3, 1.8, ((0, 8), (1, 32)), jnp.float32)
    second_out = jnp.clip(jnp.exp(math.log(0.01) - 4.6051702 * jax.random.uniform(seeds[9], (R, INNER), jnp.float32) ** block_scale(seeds[9], (R, INNER), ((0, 8), (1, 32)), -0.2, 0.2)), 0.0001, 0.01)
    return {"acts_in": acts_in, "grad_in": grad_in, "acts_out": acts_out, "grad_out": grad_out, "basis_in": basis_in, "basis_out": basis_out, "first_in": first_in, "second_in": second_in, "first_out": first_out, "second_out": second_out}


beta_one = 0.9
beta_two = 0.999
correct_one = 1.0 - 0.9 ** 10
correct_two = 1.0 - 0.999 ** 10
adam_eps = 1e-08

def adam_moments(low, first, second):
    new_first = beta_one * first + (1.0 - beta_one) * low
    new_second = beta_two * second + (1.0 - beta_two) * low * low
    direction = new_first / correct_one / (jnp.sqrt(new_second / correct_two) + adam_eps)
    return (new_first, new_second, direction.astype(jnp.bfloat16))

def reference(acts_in, grad_in, acts_out, grad_out, basis_in, basis_out, first_in, second_in, first_out, second_out):
    proj_in = jnp.dot(acts_in, basis_in, preferred_element_type=jnp.float32).astype(jnp.bfloat16)
    proj_out = jnp.dot(grad_out, basis_out, preferred_element_type=jnp.float32).astype(jnp.bfloat16)
    low_in = lax.dot_general(proj_in, grad_in, (((0,), (0,)), ((), ())), preferred_element_type=jnp.float32)
    low_out = lax.dot_general(proj_out, acts_out, (((0,), (0,)), ((), ())), preferred_element_type=jnp.float32)
    new_first_in, new_second_in, direction_in = adam_moments(low_in, first_in, second_in)
    new_first_out, new_second_out, direction_out = adam_moments(low_out, first_out, second_out)
    delta_in = jnp.dot(basis_in, direction_in, preferred_element_type=jnp.float32).astype(jnp.bfloat16)
    delta_out = lax.dot_general(direction_out, basis_out, (((0,), (1,)), ((), ())), preferred_element_type=jnp.float32).astype(jnp.bfloat16)
    return (delta_in, delta_out, new_first_in, new_second_in, new_first_out, new_second_out)
```

```python
import functools

import jax
import jax.numpy as jnp
from jax import lax
from jax.experimental import pallas as pl
from jax.experimental.pallas import tpu as pltpu
from jax.sharding import PartitionSpec as P

beta_one = 0.9
beta_two = 0.999
correct_one = 1.0 - 0.9**10
correct_two = 1.0 - 0.999**10
adam_eps = 1e-08

NX, NZ, NY = 4, 8, 4
TOK = 256
R = 256

GROUPS_Z = [[x * NZ + z for z in range(NZ)] for x in range(NX)]
GROUPS_X = [[x * NZ + z for x in range(NX)] for z in range(NZ)]
GROUPS_Y = [[y * 2 + c for y in range(NY)] for c in range(2)]

bar = lax.optimization_barrier


def adam_moments(low, first, second):
    new_first = beta_one * first + (1.0 - beta_one) * low
    new_second = beta_two * second + (1.0 - beta_two) * low * low
    direction = new_first / correct_one / (jnp.sqrt(new_second / correct_two) + adam_eps)
    return (new_first, new_second, direction.astype(jnp.bfloat16))


def shift(a, dx, dz):
    perm = [
        (x * NZ + z, (x + dx) % NX * NZ + (z + dz) % NZ) for x in range(NX) for z in range(NZ)
    ]
    return lax.ppermute(a, "mp", perm)


def other_core(a):
    return lax.ppermute(a, "dp", [(d, d ^ 1) for d in range(2 * NY)])


def gather_direct(a, axis, groups):
    n = len(groups[0])
    many = jnp.broadcast_to(a[None], (n, *a.shape))
    got = lax.all_to_all(many, axis, 0, 0, axis_index_groups=groups, tiled=True)
    return got.reshape(n * a.shape[0], *a.shape[1:])


class Piece:
    def __init__(self, array, segments):
        self.array, self.segments = array, segments

    def moved(self, dx, dz):
        return Piece(
            shift(self.array, dx, dz),
            [(p, x + dx, z + dz, r, n) for p, x, z, r, n in self.segments],
        )

    def rows(self, start, count):
        at, kept = 0, []
        for p, x, z, r, n in self.segments:
            low, high = max(at, start), min(at + n, start + count)
            if low < high:
                kept.append((p, x, z, r + low - at, high - low))
            at += n
        return Piece(self.array[start : start + count], kept)

    def halves(self):
        half = self.array.shape[0] // 2
        return self.rows(0, half), self.rows(half, half)


def stack(pieces):
    return Piece(
        jnp.concatenate([p.array for p in pieces], 0), [s for p in pieces for s in p.segments]
    )


def together(*pieces):
    arrays = bar(tuple(p.array for p in pieces))
    return [Piece(a, p.segments) for a, p in zip(arrays, pieces)]


def gather_pieces(own, partner):
    a, b = Piece(own, [(0, 0, 0, 0, TOK)]), Piece(partner, [(1, 0, 0, 0, TOK)])
    zp, zm, xp, xm = together(b.moved(0, 1), b.moved(0, -1), a.moved(1, 0), a.moved(-1, 0))
    zp2, zm2, x2a, x2b = together(
        zp.moved(0, 1), zm.moved(0, -1), xp.halves()[0].moved(1, 0), xm.halves()[1].moved(-1, 0)
    )
    four = stack([a, xp, xm, x2a, x2b])
    five = stack([b, zp, zm, zp2, zm2])
    up, down, five = together(stack([zp2, four]), stack([zm2, four]), five)
    up, down, xp, xm = together(
        up.moved(0, 1), down.moved(0, -1), five.moved(1, 0), five.moved(-1, 0)
    )
    zp3, fp = up.rows(0, TOK), up.rows(TOK, 4 * TOK)
    zm3, fm = down.rows(0, TOK), down.rows(TOK, 4 * TOK)
    early = [four, five, up, down, xp, xm]
    s = together(
        stack([zp3.halves()[0], fp]),
        stack([zm3.halves()[1], fm]),
        stack([xp.halves()[0], zp3, zm3]),
        stack([xm.halves()[1], zp3, zm3]),
    )
    u4, d4, p4, m4 = together(
        s[0].moved(0, 1), s[1].moved(0, -1), s[2].moved(1, 0), s[3].moved(-1, 0)
    )
    early += [u4, d4, p4, m4]
    h = TOK // 2
    z4 = [u4.rows(0, h), d4.rows(0, h)]
    k = 5 * h
    y3p, y3m = p4.rows(k, 2 * TOK), m4.rows(k, 2 * TOK)
    s = together(
        u4.rows(h, 4 * TOK),
        d4.rows(h, 4 * TOK),
        stack(z4 + [y3p.halves()[0]]),
        stack(z4 + [y3m.halves()[1]]),
    )
    u5, d5, p5, m5 = together(
        s[0].moved(0, 1), s[1].moved(0, -1), s[2].moved(1, 0), s[3].moved(-1, 0)
    )
    s = together(u5.halves()[0], d5.halves()[1], p5.rows(0, h), m5.rows(h, h))
    last = together(s[0].moved(0, 1), s[1].moved(0, -1), s[2].moved(1, 0), s[3].moved(-1, 0))
    return early, [u5, d5, p5, m5, *last]


def low_kernel(count, segments, blocks_ref, grads_own, grads_partner, *refs):
    pieces, start_ref, out_ref, held, arrived = refs[:count], refs[count], *refs[count + 1 :]
    copies, at = [], 0
    for index, (_, part, row, rows, _) in enumerate(segments):
        source = grads_partner if part else grads_own
        first = pl.multiple_of(blocks_ref[index] * TOK + row, 128)
        copies.append(
            pltpu.make_async_copy(
                source.at[pl.ds(first, rows)], held.at[pl.ds(at, rows)], arrived.at[index]
            )
        )
        copies[-1].start()
        at += rows
    total, at = start_ref[...], 0
    for index, (piece, _, _, rows, offset) in enumerate(segments):
        copies[index].wait()
        total += lax.dot_general(
            pieces[piece][pl.ds(offset, rows)],
            held[pl.ds(at, rows)],
            (((0,), (0,)), ((), ())),
            preferred_element_type=jnp.float32,
        )
        at += rows
    out_ref[...] = total


def low_of(pieces, grads_own, grads_partner, start):
    x, z = lax.axis_index("mp") // NZ, lax.axis_index("mp") % NZ
    segments, dxs, dzs, total = [], [], [], 0
    for index, piece in enumerate(pieces):
        offset = 0
        for part, dx, dz, row, rows in piece.segments:
            segments.append((index, part, row, rows, offset))
            dxs.append(dx)
            dzs.append(dz)
            offset += rows
            total += rows
    blocks = (x - jnp.array(dxs, jnp.int32) + NX) % NX * NZ + (
        z - jnp.array(dzs, jnp.int32) + NZ
    ) % NZ
    vmem = pl.BlockSpec(memory_space=pltpu.VMEM)
    hbm = pl.BlockSpec(memory_space=pl.ANY)
    return pl.pallas_call(
        functools.partial(low_kernel, len(pieces), segments),
        out_shape=jax.ShapeDtypeStruct((R, 256), jnp.float32),
        in_specs=[pl.BlockSpec(memory_space=pltpu.SMEM), hbm, hbm]
        + [vmem] * (len(pieces) + 1),
        out_specs=vmem,
        scratch_shapes=[
            pltpu.VMEM((total, 256), jnp.bfloat16),
            pltpu.SemaphoreType.DMA((len(segments),)),
        ],
        compiler_params=pltpu.CompilerParams(vmem_limit_bytes=40 << 20),
        cost_estimate=pl.CostEstimate(
            flops=2 * total * 256 * 256, bytes_accessed=total * 1024, transcendentals=0
        ),
    )(blocks, grads_own, grads_partner, *[p.array for p in pieces], start)


def body(
    acts_in,
    grad_in,
    acts_out,
    grad_out,
    basis_in,
    basis_out,
    first_in,
    second_in,
    first_out,
    second_out,
):
    even = lax.axis_index("dp") % 2 == 0

    def mine(a, b):
        return jnp.where(even, a, b)

    left_partner = other_core(mine(grad_out, acts_in))
    grads_partner = other_core(mine(acts_out, grad_in))
    moments_partner = other_core(
        jnp.stack([mine(first_out, first_in), mine(second_out, second_in)])
    )
    grads_own = mine(grad_in, acts_out)

    along_z = gather_direct(mine(basis_in, basis_out), "mp", GROUPS_Z)
    basis = gather_direct(along_z, "mp", GROUPS_X)
    basis_other = other_core(basis)

    def project(left):
        return jnp.dot(left, basis, preferred_element_type=jnp.float32).astype(jnp.bfloat16)

    early, late = gather_pieces(project(mine(acts_in, grad_out)), project(left_partner))
    low = low_of(early, grads_own, grads_partner, jnp.zeros((R, 256), jnp.float32))
    low = low_of(late, grads_own, grads_partner, low)

    shares = lax.all_to_all(
        low.reshape(NY, R // NY, 256), "dp", 0, 0, axis_index_groups=GROUPS_Y, tiled=True
    )
    share = shares[0] + shares[1] + shares[2] + shares[3]

    def both(own, partner):
        return mine(jnp.concatenate([own, partner]), jnp.concatenate([partner, own]))

    new_first, new_second, step = adam_moments(
        share,
        both(mine(first_in, first_out), moments_partner[0]),
        both(mine(second_in, second_out), moments_partner[1]),
    )
    h = R // NY // 2
    given = other_core(
        jnp.stack([mine(m[h:], m[:h]) for m in (new_first, new_second)])
    )
    kept = [mine(m[:h], m[h:]) for m in (new_first, new_second)]

    direction = gather_direct(step, "dp", GROUPS_Y)
    direction_other = other_core(direction)
    delta_in = jnp.dot(
        mine(basis, basis_other),
        mine(direction, direction_other),
        preferred_element_type=jnp.float32,
    )
    delta_out = lax.dot_general(
        mine(direction_other, direction),
        mine(basis_other, basis),
        (((0,), (1,)), ((), ())),
        preferred_element_type=jnp.float32,
    )
    return (
        delta_in.astype(jnp.bfloat16),
        delta_out.astype(jnp.bfloat16),
        mine(kept[0], given[0]),
        mine(kept[1], given[1]),
        mine(given[0], kept[0]),
        mine(given[1], kept[1]),
    )


def solution(mesh):
    in_specs = (
        P(("dp", "mp"), None),
        P("dp", "mp"),
        P("dp", "mp"),
        P(("dp", "mp"), None),
        P("mp", None),
        P("mp", None),
        P("dp", "mp"),
        P("dp", "mp"),
        P("dp", "mp"),
        P("dp", "mp"),
    )
    out_specs = (
        P(None, "mp"),
        P("mp", None),
        P("dp", "mp"),
        P("dp", "mp"),
        P("dp", "mp"),
        P("dp", "mp"),
    )
    return jax.shard_map(body, mesh=mesh, in_specs=in_specs, out_specs=out_specs, check_vma=False)
```

```python
import functools

import jax
import jax.numpy as jnp
from jax import lax
from jax.experimental import pallas as pl
from jax.experimental.pallas import tpu as pltpu
from jax.sharding import PartitionSpec as P

beta_one = 0.9
beta_two = 0.999
correct_one = 1.0 - 0.9**10
correct_two = 1.0 - 0.999**10
adam_eps = 1e-08

NX, NZ, NY = 4, 8, 4
TOK = 256
SEG = 128
PART = TOK // SEG
R = 256

GROUPS_Z = [[x * NZ + z for z in range(NZ)] for x in range(NX)]
GROUPS_X = [[x * NZ + z for x in range(NX)] for z in range(NZ)]

bar = lax.optimization_barrier


def adam_moments(low, first, second):
    new_first = beta_one * first + (1.0 - beta_one) * low
    new_second = beta_two * second + (1.0 - beta_two) * low * low
    direction = new_first / correct_one / (jnp.sqrt(new_second / correct_two) + adam_eps)
    return (new_first, new_second, direction.astype(jnp.bfloat16))


def shift(a, dx, dz):
    perm = [
        (x * NZ + z, (x + dx) % NX * NZ + (z + dz) % NZ) for x in range(NX) for z in range(NZ)
    ]
    return lax.ppermute(a, "mp", perm)


def other_core(a):
    return lax.ppermute(a, "dp", [(d, d ^ 1) for d in range(2 * NY)])


def gather_direct(a, axis, groups=None):
    n = len(groups[0]) if groups else lax.axis_size(axis)
    many = jnp.broadcast_to(a[None], (n, *a.shape))
    got = lax.all_to_all(many, axis, 0, 0, axis_index_groups=groups, tiled=True)
    return got.reshape(n * a.shape[0], *a.shape[1:])


class Piece:
    def __init__(self, array, segments):
        self.array, self.segments = array, segments

    def moved(self, dx, dz):
        return Piece(
            shift(self.array, dx, dz), [(p, x + dx, z + dz, k) for p, x, z, k in self.segments]
        )

    def cut(self, start, count):
        return Piece(self.array[start : start + count], self.segments[start : start + count])

    def halves(self):
        half = len(self.segments) // 2
        return self.cut(0, half), self.cut(half, half)


def stack(pieces):
    return Piece(
        jnp.concatenate([p.array for p in pieces], 0), [s for p in pieces for s in p.segments]
    )


def together(*pieces):
    arrays = bar(tuple(p.array for p in pieces))
    return [Piece(a, p.segments) for a, p in zip(arrays, pieces)]


def with_low(pieces, low):
    *arrays, low = bar((*[p.array for p in pieces], low))
    return [Piece(a, p.segments) for a, p in zip(arrays, pieces)], low


def gather_low(proj_in, proj_out, add):
    n = PART
    a, b = (Piece(array, [(part, 0, 0, k) for k in range(n)]) for part, array in enumerate((proj_in, proj_out)))
    zp, zm, xp, xm = together(b.moved(0, 1), b.moved(0, -1), a.moved(1, 0), a.moved(-1, 0))
    zp2, zm2, x2a, x2b = together(
        zp.moved(0, 1), zm.moved(0, -1), xp.halves()[0].moved(1, 0), xm.halves()[1].moved(-1, 0)
    )
    four = [a, xp, xm, x2a, x2b]
    up, down, side = together(
        stack([zp2, *four]), stack([zm2, *four]), stack([b, zp, zm, zp2, zm2])
    )
    sent = [Piece(up.array, [None] * n + up.segments[n:]), side]
    up, down, xp5, xm5 = together(
        up.moved(0, 1), down.moved(0, -1), side.moved(1, 0), side.moved(-1, 0)
    )
    low = add(sent, None)
    zp3, fp = up.cut(0, n), up.cut(n, 4 * n)
    zm3, fm = down.cut(0, n), down.cut(n, 4 * n)
    s, low = with_low(
        [
            stack([zp3.halves()[0], fp]),
            stack([zm3.halves()[1], fm]),
            stack([xp5.halves()[0], zp3, zm3]),
            stack([xm5.halves()[1], zp3, zm3]),
        ],
        low,
    )
    u4, d4, p4, m4 = together(
        s[0].moved(0, 1), s[1].moved(0, -1), s[2].moved(1, 0), s[3].moved(-1, 0)
    )
    low = add([up, down, xp5, xm5], low)
    h = n // 2
    u4a, d4a = u4.cut(0, h), d4.cut(0, h)
    y3p, y3m = p4.cut(5 * h, 2 * n), m4.cut(5 * h, 2 * n)
    s, low = with_low(
        [
            u4.cut(h, 4 * n),
            d4.cut(h, 4 * n),
            stack([u4a, d4a, y3p.halves()[0]]),
            stack([u4a, d4a, y3m.halves()[1]]),
        ],
        low,
    )
    u5, d5, p5, m5 = together(
        s[0].moved(0, 1), s[1].moved(0, -1), s[2].moved(1, 0), s[3].moved(-1, 0)
    )
    low = add([u4, d4, p4, m4], low)
    s, low = with_low([u5.halves()[0], d5.halves()[1], p5.cut(0, h), m5.cut(h, h)], low)
    last = together(s[0].moved(0, 1), s[1].moved(0, -1), s[2].moved(1, 0), s[3].moved(-1, 0))
    low = add([u5, d5, p5, m5], low)
    return add(last, low)


def low_kernel(count, runs, has_start, table, grad_in, acts_out, *refs):
    pieces, (out_ref, held, arrived) = refs[:count], refs[-3:]
    copies, at = [], 0
    for index, (_, _, part, first, segments) in enumerate(runs):
        row = pl.multiple_of(table[index] * TOK + first * SEG, SEG)
        rows = segments * SEG
        copies.append(
            pltpu.make_async_copy(
                (grad_in, acts_out)[part].at[pl.ds(row, rows)],
                held.at[pl.ds(at, rows)],
                arrived.at[index],
            )
        )
        copies[-1].start()
        at += rows
    totals = [refs[count][:, part].reshape(R, 256) if has_start else None for part in (0, 1)]
    at, index = 0, 0
    while index < len(runs):
        left, (piece, _, part, _, _), rows = [], runs[index], 0
        while index < len(runs) and (runs[index][0], runs[index][2]) == (piece, part):
            _, offset, _, _, segments = runs[index]
            copies[index].wait()
            left += [pieces[piece][offset + k] for k in range(segments)]
            rows += segments * SEG
            index += 1
        left = jnp.concatenate(left, 1) if len(left) > 1 else left[0]
        product = jnp.dot(left, held[pl.ds(at, rows)], preferred_element_type=jnp.float32)
        totals[part] = product if totals[part] is None else totals[part] + product
        at += rows
    for part in (0, 1):
        out_ref[:, part] = totals[part].reshape(out_ref.shape[0], -1, 256)


def low_of(grads, pieces, start):
    x, z = lax.axis_index("mp") // NZ, lax.axis_index("mp") % NZ
    runs, dxs, dzs = [], [], []
    for index, piece in enumerate(pieces):
        for offset, segment in enumerate(piece.segments):
            if segment is None:
                continue
            part, dx, dz, k = segment
            joins = (
                runs
                and runs[-1][0] == index
                and runs[-1][2] == part
                and (dxs[-1], dzs[-1]) == (dx, dz)
                and runs[-1][3] + runs[-1][4] == k
            )
            if joins:
                runs[-1] = (*runs[-1][:4], runs[-1][4] + 1)
            else:
                runs.append((index, offset, part, k, 1))
                dxs.append(dx)
                dzs.append(dz)
    rows = SEG * sum(run[4] for run in runs)
    blocks = (x - jnp.array(dxs, jnp.int32) + NX) % NX * NZ + (
        z - jnp.array(dzs, jnp.int32) + NZ
    ) % NZ
    vmem = pl.BlockSpec(memory_space=pltpu.VMEM)
    starts = [] if start is None else [start]
    return pl.pallas_call(
        functools.partial(low_kernel, len(pieces), runs, bool(starts)),
        out_shape=jax.ShapeDtypeStruct((2 * NY, 2, R // NY // 2, 256), jnp.float32),
        in_specs=[pl.BlockSpec(memory_space=pltpu.SMEM)]
        + [pl.BlockSpec(memory_space=pltpu.HBM)] * 2
        + [vmem] * (len(pieces) + len(starts)),
        out_specs=vmem,
        scratch_shapes=[
            pltpu.VMEM((rows, 256), jnp.bfloat16),
            pltpu.SemaphoreType.DMA((len(runs),)),
        ],
        compiler_params=pltpu.CompilerParams(vmem_limit_bytes=16 << 20),
        cost_estimate=pl.CostEstimate(
            flops=2 * rows * R * 256, bytes_accessed=rows * 1024, transcendentals=0
        ),
    )(blocks, *grads, *[p.array for p in pieces], *starts)


def project_kernel(core, acts_in, grad_out, basis_own, basis_other, *outs):
    def run(bases):
        for left, basis, out in zip((acts_in, grad_out), bases, outs):
            proj = jnp.dot(left[...], basis[...], preferred_element_type=jnp.float32)
            proj = proj.T.astype(jnp.bfloat16)
            for j in range(PART):
                out[j] = proj[:, j * SEG : (j + 1) * SEG]

    @pl.when(core[0] == 0)
    def _():
        run((basis_own, basis_other))

    @pl.when(core[0] == 1)
    def _():
        run((basis_other, basis_own))


def project(core, acts_in, grad_out, basis_own, basis_other):
    vmem = pl.BlockSpec(memory_space=pltpu.VMEM)
    return pl.pallas_call(
        project_kernel,
        out_shape=[jax.ShapeDtypeStruct((PART, R, SEG), jnp.bfloat16)] * 2,
        in_specs=[pl.BlockSpec(memory_space=pltpu.SMEM)] + [vmem] * 4,
        out_specs=[vmem] * 2,
        compiler_params=pltpu.CompilerParams(vmem_limit_bytes=16 << 20),
        cost_estimate=pl.CostEstimate(
            flops=4 * TOK * acts_in.shape[1] * R, bytes_accessed=8 << 20, transcendentals=0
        ),
    )(core[None], acts_in, grad_out, basis_own, basis_other)


def body(
    acts_in,
    grad_in,
    acts_out,
    grad_out,
    basis_in,
    basis_out,
    first_in,
    second_in,
    first_out,
    second_out,
):
    core = lax.axis_index("dp") % 2

    def mine(a, b):
        return jnp.where(core == 0, a, b)

    along_z = gather_direct(mine(basis_in, basis_out), "mp", GROUPS_Z)
    basis_own = gather_direct(along_z, "mp", GROUPS_X)
    basis_other = other_core(basis_own)
    low = gather_low(
        *project(core, acts_in, grad_out, basis_own, basis_other),
        functools.partial(low_of, (grad_in, acts_out)),
    )
    shares = lax.all_to_all(low, "dp", 0, 0, tiled=True)
    share = functools.reduce(jnp.add, [shares[d] for d in range(shares.shape[0])])
    new_first_in, new_second_in, step_in = adam_moments(share[0], first_in, second_in)
    new_first_out, new_second_out, step_out = adam_moments(share[1], first_out, second_out)
    steps = gather_direct(jnp.stack([step_in, step_out])[None], "dp")
    delta_in = jnp.dot(
        mine(basis_own, basis_other),
        steps[:, 0].reshape(R, 256),
        preferred_element_type=jnp.float32,
    )
    delta_out = lax.dot_general(
        steps[:, 1].reshape(R, 256),
        mine(basis_other, basis_own),
        (((0,), (1,)), ((), ())),
        preferred_element_type=jnp.float32,
    )
    return (
        delta_in.astype(jnp.bfloat16),
        delta_out.astype(jnp.bfloat16),
        new_first_in,
        new_second_in,
        new_first_out,
        new_second_out,
    )


def solution(mesh):
    in_specs = (
        P(("dp", "mp"), None),
        P("dp", "mp"),
        P("dp", "mp"),
        P(("dp", "mp"), None),
        P("mp", None),
        P("mp", None),
        P("dp", "mp"),
        P("dp", "mp"),
        P("dp", "mp"),
        P("dp", "mp"),
    )
    out_specs = (
        P(None, "mp"),
        P("mp", None),
        P("dp", "mp"),
        P("dp", "mp"),
        P("dp", "mp"),
        P("dp", "mp"),
    )
    return jax.shard_map(body, mesh=mesh, in_specs=in_specs, out_specs=out_specs, check_vma=False)
```

```python
import functools

import jax
import jax.numpy as jnp
from jax import lax
from jax.experimental import pallas as pl
from jax.experimental.pallas import tpu as pltpu
from jax.sharding import PartitionSpec as P

beta_one = 0.9
beta_two = 0.999
correct_one = 1.0 - 0.9**10
correct_two = 1.0 - 0.999**10
adam_eps = 1e-08

NX, NZ, NY = 4, 8, 4
TOK = 256
SEG = 128
PART = TOK // SEG
R = 256

GROUPS_Z = [[x * NZ + z for z in range(NZ)] for x in range(NX)]
GROUPS_Y = [[y * 2 + c for y in range(NY)] for c in range(2)]
GROUPS_X = [[x * NZ + z for x in range(NX)] for z in range(NZ)]

bar = lax.optimization_barrier


def adam_moments(low, first, second):
    new_first = beta_one * first + (1.0 - beta_one) * low
    new_second = beta_two * second + (1.0 - beta_two) * low * low
    direction = new_first / correct_one / (jnp.sqrt(new_second / correct_two) + adam_eps)
    return (new_first, new_second, direction.astype(jnp.bfloat16))


def shift(a, dx, dz):
    perm = [
        (x * NZ + z, (x + dx) % NX * NZ + (z + dz) % NZ) for x in range(NX) for z in range(NZ)
    ]
    return lax.ppermute(a, "mp", perm)


def other_core(a):
    return lax.ppermute(a, "dp", [(d, d ^ 1) for d in range(2 * NY)])


def gather_direct(a, axis, groups=None):
    n = len(groups[0]) if groups else lax.axis_size(axis)
    many = jnp.broadcast_to(a[None], (n, *a.shape))
    got = lax.all_to_all(many, axis, 0, 0, axis_index_groups=groups, tiled=True)
    return got.reshape(n * a.shape[0], *a.shape[1:])


class Piece:
    def __init__(self, array, segments):
        self.array, self.segments = array, segments

    def moved(self, dx, dz):
        return Piece(
            shift(self.array, dx, dz), [(p, x + dx, z + dz, k) for p, x, z, k in self.segments]
        )

    def cut(self, start, count):
        return Piece(self.array[start : start + count], self.segments[start : start + count])

    def halves(self):
        half = len(self.segments) // 2
        return self.cut(0, half), self.cut(half, half)


def pack_kernel(layout, *refs):
    count = 1 + max(source for packed in layout for source, _, _ in packed)
    for packed, out in zip(layout, refs[count:]):
        at = 0
        for source, start, segments in packed:
            out[at : at + segments] = refs[source][start : start + segments]
            at += segments


def pack(sources, layout):
    vmem = pl.BlockSpec(memory_space=pltpu.VMEM)
    sizes = [sum(run[2] for run in packed) for packed in layout]
    arrays = pl.pallas_call(
        functools.partial(pack_kernel, layout),
        out_shape=[jax.ShapeDtypeStruct((size, R, SEG), jnp.bfloat16) for size in sizes],
        in_specs=[vmem] * len(sources),
        out_specs=[vmem] * len(layout),
        compiler_params=pltpu.CompilerParams(vmem_limit_bytes=20 << 20),
    )(*[p.array for p in sources])
    return [
        Piece(array, [s for source, at, n in packed for s in sources[source].segments[at : at + n]])
        for array, packed in zip(arrays, layout)
    ]


def stack(pieces):
    return Piece(
        jnp.concatenate([p.array for p in pieces], 0), [s for p in pieces for s in p.segments]
    )


def together(*pieces):
    arrays = bar(tuple(p.array for p in pieces))
    return [Piece(a, p.segments) for a, p in zip(arrays, pieces)]


def with_low(pieces, low):
    *arrays, low = bar((*[p.array for p in pieces], low))
    return [Piece(a, p.segments) for a, p in zip(arrays, pieces)], low


def gather_low(proj_in, proj_out, add):
    n = PART
    a, b = (Piece(array, [(part, 0, 0, k) for k in range(n)]) for part, array in enumerate((proj_in, proj_out)))
    zp, zm, xp, xm = together(b.moved(0, 1), b.moved(0, -1), a.moved(1, 0), a.moved(-1, 0))
    zp2, zm2, x2a, x2b = together(
        zp.moved(0, 1), zm.moved(0, -1), xp.halves()[0].moved(1, 0), xm.halves()[1].moved(-1, 0)
    )
    h = n // 2
    four = [(0, 0, n), (1, 0, n), (2, 0, n), (3, 0, h), (4, 0, h)]
    up, down, side = pack(
        [a, xp, xm, x2a, x2b, b, zp, zm, zp2, zm2],
        [
            [(8, 0, n), *four],
            [(9, 0, n), *four],
            [(k, 0, n) for k in range(5, 10)],
        ],
    )
    sent = [Piece(up.array, [None] * n + up.segments[n:]), side]
    up, down, xp5, xm5 = together(
        up.moved(0, 1), down.moved(0, -1), side.moved(1, 0), side.moved(-1, 0)
    )
    low = add(sent, None)
    (up, down, xp5, xm5), low = with_low([up, down, xp5, xm5], low)
    s = pack(
        [up, down, xp5, xm5],
        [
            [(0, 0, h), (0, n, 4 * n)],
            [(1, h, h), (1, n, 4 * n)],
            [(2, 0, 5 * h), (0, 0, n), (1, 0, n)],
            [(3, 5 * h, 5 * h), (0, 0, n), (1, 0, n)],
        ],
    )
    u4, d4, p4, m4 = together(
        s[0].moved(0, 1), s[1].moved(0, -1), s[2].moved(1, 0), s[3].moved(-1, 0)
    )
    low = add([up, down, xp5, xm5], low)
    z4 = stack([u4.cut(0, h), d4.cut(0, h)])
    y3p, y3m = p4.cut(5 * h, 2 * n), m4.cut(5 * h, 2 * n)
    s, low = with_low(
        [
            u4.cut(h, 4 * n),
            d4.cut(h, 4 * n),
            stack([z4, y3p.halves()[0]]),
            stack([z4, y3m.halves()[1]]),
            z4,
        ],
        low,
    )
    u5, d5, p5, m5, q5 = together(
        s[0].moved(0, 1), s[1].moved(0, -1), s[2].moved(1, 0), s[3].moved(-1, 0), s[4].moved(2, 0)
    )
    low = add([u4, d4, p4, m4], low)
    s, low = with_low([u5.halves()[0], d5.halves()[1]], low)
    last = together(s[0].moved(0, 1), s[1].moved(0, -1))
    low = add([u5, d5, p5, m5, q5], low)
    return add(last, low, True)


def both_ways(core, run, own, other):
    @pl.when(core == 0)
    def _():
        run(own, other)

    @pl.when(core == 1)
    def _():
        run(other, own)


def low_kernel(count, runs, has_start, last, table, grad_in, acts_out, *refs):
    pieces, out_ref = refs[:count], refs[-2 if last else -1]
    totals = [refs[count][:, part].reshape(R, 256) if has_start else None for part in (0, 1)]
    for index, (piece, offset, part, first, segments) in enumerate(runs):
        left = [pieces[piece][offset + k] for k in range(segments)]
        left = jnp.concatenate(left, 1) if segments > 1 else left[0]
        row = pl.multiple_of(table[index] * TOK + first * SEG, SEG)
        right = (grad_in, acts_out)[part][pl.ds(row, segments * SEG)]
        product = jnp.dot(left, right, preferred_element_type=jnp.float32)
        totals[part] = product if totals[part] is None else totals[part] + product
    if not last:
        for part in (0, 1):
            out_ref[:, part] = totals[part].reshape(out_ref.shape[0], -1, 256)
        return

    def split(keep, give):
        for part in (0, 1):
            rows = totals[part].reshape(NY, 2, -1, 256)
            keep[:, part], give[:, part] = rows[:, 0], rows[:, 1]

    both_ways(table[len(runs)], split, refs[-2], refs[-1])


def low_of(grads, core, pieces, start, last=False):
    x, z = lax.axis_index("mp") // NZ, lax.axis_index("mp") % NZ
    runs, dxs, dzs = [], [], []
    for index, piece in enumerate(pieces):
        for offset, segment in enumerate(piece.segments):
            if segment is None:
                continue
            part, dx, dz, k = segment
            joins = (
                runs
                and runs[-1][0] == index
                and runs[-1][2] == part
                and (dxs[-1], dzs[-1]) == (dx, dz)
                and runs[-1][3] + runs[-1][4] == k
            )
            if joins:
                runs[-1] = (*runs[-1][:4], runs[-1][4] + 1)
            else:
                runs.append((index, offset, part, k, 1))
                dxs.append(dx)
                dzs.append(dz)
    rows = SEG * sum(run[4] for run in runs)
    blocks = (x - jnp.array(dxs, jnp.int32) + NX) % NX * NZ + (
        z - jnp.array(dzs, jnp.int32) + NZ
    ) % NZ
    vmem = pl.BlockSpec(memory_space=pltpu.VMEM)
    starts = [] if start is None else [start]
    return pl.pallas_call(
        functools.partial(low_kernel, len(pieces), runs, bool(starts), last),
        out_shape=[jax.ShapeDtypeStruct((NY, 2, R // NY // 2, 256), jnp.float32)] * 2
        if last
        else jax.ShapeDtypeStruct((2 * NY, 2, R // NY // 2, 256), jnp.float32),
        in_specs=[pl.BlockSpec(memory_space=pltpu.SMEM)]
        + [vmem] * (2 + len(pieces) + len(starts)),
        out_specs=[vmem] * 2 if last else vmem,
        compiler_params=pltpu.CompilerParams(vmem_limit_bytes=20 << 20),
        cost_estimate=pl.CostEstimate(
            flops=2 * rows * R * 256, bytes_accessed=rows * 1024, transcendentals=0
        ),
    )(jnp.append(blocks, core), *grads, *[p.array for p in pieces], *starts)


def spread_along_x(own):
    h = own.shape[0] // 2
    ahead, behind = shift(own, 1, 0), shift(own, -1, 0)
    own_other = other_core(own)
    ahead, behind, own_other = bar((ahead, behind, own_other))
    far = shift(ahead[:h], 1, 0), shift(behind[h:], -1, 0)
    near_other = other_core(ahead), other_core(behind)
    places = [(0, 0), (1, 0), (-1, 0), (2, 0), (2, h)]
    arrays = [own, ahead, behind, *far]
    others = [own_other, *near_other, *[other_core(f) for f in far]]
    return [(a, *p) for a, p in zip(arrays, places)], [(a, *p) for a, p in zip(others, places)]


def project_kernel(firsts, count, table, acts_in, grad_out, *refs):
    own, other, outs = refs[:count], refs[count : 2 * count], refs[2 * count : -2]
    held, arrived = refs[-2:]
    sizes = [part.shape[0] for part in own]
    copies = []
    for side, left in enumerate((acts_in, grad_out)):
        for k, size in enumerate(sizes):
            here = pl.multiple_of(table[1 + k] * (NZ * SEG) + firsts[k], SEG)
            copies.append(
                pltpu.make_async_copy(
                    left.at[:, pl.ds(here, size)],
                    held.at[side, :, pl.ds(sum(sizes[:k]), size)],
                    arrived.at[side, k],
                )
            )
            copies[-1].start()

    def run(*bases):
        for side, (parts, out) in enumerate(zip(bases, outs)):
            proj = None
            for k, part in enumerate(parts):
                copies[side * count + k].wait()
                at = sum(sizes[:k])
                product = jnp.dot(
                    held[side, :, at : at + sizes[k]], part[...], preferred_element_type=jnp.float32
                )
                proj = product if proj is None else proj + product
            proj = proj.T.astype(jnp.bfloat16)
            for j in range(PART):
                out[j] = proj[:, j * SEG : (j + 1) * SEG]

    both_ways(table[0], run, own, other)


def delta_kernel(firsts, count, table, steps, *refs):
    own, other = refs[:count], refs[count : 2 * count]
    delta_in, delta_out, held_in, held_out, left = refs[2 * count :]

    def run(parts_in, parts_out):
        copies = []

        def send(source, target, k):
            copies.append(pltpu.make_async_copy(source, target, left.at[len(copies)]))
            copies[-1].start()

        step = steps[:, 0].reshape(R, 256)
        for k, part in enumerate(parts_in):
            rows = part.shape[0]
            here = pl.ds(pl.multiple_of(table[1 + k] * (NZ * SEG) + firsts[k], SEG), rows)
            delta = jnp.dot(part[...], step, preferred_element_type=jnp.float32)
            held_in[here] = delta.astype(jnp.bfloat16)
            send(held_in.at[here], delta_in.at[here], k)
        step = steps[:, 1].reshape(R, 256).T
        for k, part in enumerate(parts_out):
            rows = part.shape[0]
            here = pl.ds(pl.multiple_of(table[1 + k] * (NZ * SEG) + firsts[k], SEG), rows)
            delta = lax.dot_general(
                step, part[...], (((1,), (1,)), ((), ())), preferred_element_type=jnp.float32
            )
            held_out[:, here] = delta.astype(jnp.bfloat16)
            send(held_out.at[:, here], delta_out.at[:, here], k)
        for copy in copies:
            copy.wait()

    both_ways(table[0], run, own, other)


def with_bases(kernel, out_shape, out_specs, scratch, flops, space, table, operands, own, other):
    vmem = pl.BlockSpec(memory_space=pltpu.VMEM)
    arrays = [a for a, _, _ in own + other]
    return pl.pallas_call(
        functools.partial(kernel, [first for _, _, first in own], len(own)),
        out_shape=out_shape,
        in_specs=[pl.BlockSpec(memory_space=pltpu.SMEM)]
        + [pl.BlockSpec(memory_space=space)] * len(operands)
        + [vmem] * len(arrays),
        out_specs=out_specs,
        scratch_shapes=scratch,
        compiler_params=pltpu.CompilerParams(vmem_limit_bytes=48 << 20),
        cost_estimate=pl.CostEstimate(flops=flops, bytes_accessed=8 << 20, transcendentals=0),
    )(table, *operands, *arrays)


def project(table, acts_in, grad_out, own, other):
    return with_bases(
        project_kernel,
        [jax.ShapeDtypeStruct((PART, R, SEG), jnp.bfloat16)] * 2,
        [pl.BlockSpec(memory_space=pltpu.VMEM)] * 2,
        [
            pltpu.VMEM((2, *acts_in.shape), jnp.bfloat16),
            pltpu.SemaphoreType.DMA((2, len(own))),
        ],
        4 * TOK * acts_in.shape[1] * R,
        pl.ANY,
        table,
        [acts_in, grad_out],
        own,
        other,
    )


def deltas(table, steps, own, other):
    width = NX * NZ * SEG
    shapes = [(width, 256), (256, width)]
    return with_bases(
        delta_kernel,
        [jax.ShapeDtypeStruct(shape, jnp.bfloat16) for shape in shapes],
        [pl.BlockSpec(memory_space=pl.ANY)] * 2,
        [pltpu.VMEM(shape, jnp.bfloat16) for shape in shapes]
        + [pltpu.SemaphoreType.DMA((2 * len(own),))],
        4 * 256 * width * R,
        pltpu.VMEM,
        table,
        [steps],
        own,
        other,
    )


def body(
    acts_in,
    grad_in,
    acts_out,
    grad_out,
    basis_in,
    basis_out,
    first_in,
    second_in,
    first_out,
    second_out,
):
    core = lax.axis_index("dp") % 2

    def mine(a, b):
        return jnp.where(core == 0, a, b)

    along_z = gather_direct(mine(basis_in, basis_out), "mp", GROUPS_Z)
    own, other = spread_along_x(along_z)
    x = lax.axis_index("mp") // NZ
    table = jnp.stack([core] + [(x - dx + NX) % NX for _, dx, _ in own])
    keep, give = gather_low(
        *project(table, acts_in, grad_out, own, other),
        functools.partial(low_of, (grad_in, acts_out), core),
    )
    shares = lax.all_to_all(
        keep + other_core(give), "dp", 0, 0, axis_index_groups=GROUPS_Y, tiled=True
    )
    share = (shares[0] + shares[1]) + (shares[2] + shares[3])
    new_first_in, new_second_in, step_in = adam_moments(share[0], first_in, second_in)
    new_first_out, new_second_out, step_out = adam_moments(share[1], first_out, second_out)
    steps = gather_direct(jnp.stack([step_in, step_out])[None], "dp")
    delta_in, delta_out = deltas(table, steps, own, other)
    return (
        delta_in,
        delta_out,
        new_first_in,
        new_second_in,
        new_first_out,
        new_second_out,
    )


def solution(mesh):
    in_specs = (
        P(("dp", "mp"), None),
        P("dp", "mp"),
        P("dp", "mp"),
        P(("dp", "mp"), None),
        P("mp", None),
        P("mp", None),
        P("dp", "mp"),
        P("dp", "mp"),
        P("dp", "mp"),
        P("dp", "mp"),
    )
    out_specs = (
        P(None, "mp"),
        P("mp", None),
        P("dp", "mp"),
        P("dp", "mp"),
        P("dp", "mp"),
        P("dp", "mp"),
    )
    return jax.shard_map(body, mesh=mesh, in_specs=in_specs, out_specs=out_specs, check_vma=False)
```

```python
import functools

import jax
import jax.numpy as jnp
from jax import lax
from jax.experimental import pallas as pl
from jax.experimental.pallas import tpu as pltpu
from jax.sharding import PartitionSpec as P

beta_one = 0.9
beta_two = 0.999
correct_one = 1.0 - 0.9**10
correct_two = 1.0 - 0.999**10
adam_eps = 1e-08

NX, NZ, NY = 4, 8, 4
TOK = 256
SEG = 128
PART = TOK // SEG
R = 256

GROUPS_Z = [[x * NZ + z for z in range(NZ)] for x in range(NX)]
GROUPS_Y = [[y * 2 + c for y in range(NY)] for c in range(2)]
GROUPS_X = [[x * NZ + z for x in range(NX)] for z in range(NZ)]

bar = lax.optimization_barrier


def adam_moments(low, first, second):
    new_first = beta_one * first + (1.0 - beta_one) * low
    new_second = beta_two * second + (1.0 - beta_two) * low * low
    direction = new_first / correct_one / (jnp.sqrt(new_second / correct_two) + adam_eps)
    return (new_first, new_second, direction.astype(jnp.bfloat16))


def shift(a, dx, dz):
    perm = [
        (x * NZ + z, (x + dx) % NX * NZ + (z + dz) % NZ) for x in range(NX) for z in range(NZ)
    ]
    return lax.ppermute(a, "mp", perm)


def other_core(a):
    return lax.ppermute(a, "dp", [(d, d ^ 1) for d in range(2 * NY)])


def gather_direct(a, axis, groups=None):
    n = len(groups[0]) if groups else lax.axis_size(axis)
    many = jnp.broadcast_to(a[None], (n, *a.shape))
    got = lax.all_to_all(many, axis, 0, 0, axis_index_groups=groups, tiled=True)
    return got.reshape(n * a.shape[0], *a.shape[1:])


class Piece:
    def __init__(self, array, segments):
        self.array, self.segments = array, segments

    def moved(self, dx, dz):
        return Piece(
            shift(self.array, dx, dz), [(p, x + dx, z + dz, k) for p, x, z, k in self.segments]
        )

    def cut(self, start, count):
        return Piece(self.array[start : start + count], self.segments[start : start + count])

    def halves(self):
        half = len(self.segments) // 2
        return self.cut(0, half), self.cut(half, half)


def pack_kernel(layout, *refs):
    count = 1 + max(source for packed in layout for source, _, _ in packed)
    for packed, out in zip(layout, refs[count:]):
        at = 0
        for source, start, segments in packed:
            out[at : at + segments] = refs[source][start : start + segments]
            at += segments


def pack(sources, layout):
    vmem = pl.BlockSpec(memory_space=pltpu.VMEM)
    sizes = [sum(run[2] for run in packed) for packed in layout]
    arrays = pl.pallas_call(
        functools.partial(pack_kernel, layout),
        out_shape=[jax.ShapeDtypeStruct((size, R, SEG), jnp.bfloat16) for size in sizes],
        in_specs=[vmem] * len(sources),
        out_specs=[vmem] * len(layout),
        compiler_params=pltpu.CompilerParams(vmem_limit_bytes=20 << 20),
    )(*[p.array for p in sources])
    return [
        Piece(array, [s for source, at, n in packed for s in sources[source].segments[at : at + n]])
        for array, packed in zip(arrays, layout)
    ]


def stack(pieces):
    return Piece(
        jnp.concatenate([p.array for p in pieces], 0), [s for p in pieces for s in p.segments]
    )


def together(*pieces):
    arrays = bar(tuple(p.array for p in pieces))
    return [Piece(a, p.segments) for a, p in zip(arrays, pieces)]


def with_low(pieces, low):
    *arrays, low = bar((*[p.array for p in pieces], low))
    return [Piece(a, p.segments) for a, p in zip(arrays, pieces)], low


def gather_low(proj_in, proj_out, add):
    n = PART
    a, b = (Piece(array, [(part, 0, 0, k) for k in range(n)]) for part, array in enumerate((proj_in, proj_out)))
    zp, zm, xp, xm = together(b.moved(0, 1), b.moved(0, -1), a.moved(1, 0), a.moved(-1, 0))
    zp2, zm2, x2a, x2b = together(
        zp.moved(0, 1), zm.moved(0, -1), xp.halves()[0].moved(1, 0), xm.halves()[1].moved(-1, 0)
    )
    h = n // 2
    four = [(0, 0, n), (1, 0, n), (2, 0, n), (3, 0, h), (4, 0, h)]
    up, down, side = pack(
        [a, xp, xm, x2a, x2b, b, zp, zm, zp2, zm2],
        [
            [(8, 0, n), *four],
            [(9, 0, n), *four],
            [(k, 0, n) for k in range(5, 10)],
        ],
    )
    sent = [Piece(up.array, [None] * n + up.segments[n:]), side]
    up, down, xp5, xm5 = together(
        up.moved(0, 1), down.moved(0, -1), side.moved(1, 0), side.moved(-1, 0)
    )
    low = add(sent, None)
    (up, down, xp5, xm5), low = with_low([up, down, xp5, xm5], low)
    s = pack(
        [up, down, xp5, xm5],
        [
            [(0, 0, h), (0, n, 4 * n)],
            [(1, h, h), (1, n, 4 * n)],
            [(2, 0, 5 * h), (0, 0, n), (1, 0, n)],
            [(3, 5 * h, 5 * h), (0, 0, n), (1, 0, n)],
        ],
    )
    u4, d4, p4, m4 = together(
        s[0].moved(0, 1), s[1].moved(0, -1), s[2].moved(1, 0), s[3].moved(-1, 0)
    )
    low = add([up, down, xp5, xm5], low)
    z4 = stack([u4.cut(0, h), d4.cut(0, h)])
    y3p, y3m = p4.cut(5 * h, 2 * n), m4.cut(5 * h, 2 * n)
    s, low = with_low(
        [
            u4.cut(h, 4 * n),
            d4.cut(h, 4 * n),
            stack([z4, y3p.halves()[0]]),
            stack([z4, y3m.halves()[1]]),
            z4,
        ],
        low,
    )
    u5, d5, p5, m5, q5 = together(
        s[0].moved(0, 1), s[1].moved(0, -1), s[2].moved(1, 0), s[3].moved(-1, 0), s[4].moved(2, 0)
    )
    low = add([u4, d4, p4, m4], low)
    s, low = with_low([u5.halves()[0], d5.halves()[1]], low)
    last = together(s[0].moved(0, 1), s[1].moved(0, -1))
    low = add([u5, d5, p5, m5, q5], low)
    return add(last, low, True)


def both_ways(core, run, own, other):
    @pl.when(core == 0)
    def _():
        run(own, other)

    @pl.when(core == 1)
    def _():
        run(other, own)


def low_kernel(count, runs, has_start, last, table, grad_in, acts_out, *refs):
    pieces, out_ref = refs[:count], refs[-2 if last else -1]
    totals = [refs[count][:, part].reshape(R, 256) if has_start else None for part in (0, 1)]
    for index, (piece, offset, part, first, segments) in enumerate(runs):
        left = [pieces[piece][offset + k] for k in range(segments)]
        left = jnp.concatenate(left, 1) if segments > 1 else left[0]
        row = pl.multiple_of(table[index] * TOK + first * SEG, SEG)
        right = (grad_in, acts_out)[part][pl.ds(row, segments * SEG)]
        product = jnp.dot(left, right, preferred_element_type=jnp.float32)
        totals[part] = product if totals[part] is None else totals[part] + product
    if not last:
        for part in (0, 1):
            out_ref[:, part] = totals[part].reshape(out_ref.shape[0], -1, 256)
        return

    def split(keep, give):
        for part in (0, 1):
            rows = totals[part].reshape(NY, 2, -1, 256)
            keep[:, part], give[:, part] = rows[:, 0], rows[:, 1]

    both_ways(table[len(runs)], split, refs[-2], refs[-1])


def low_of(grads, core, pieces, start, last=False):
    x, z = lax.axis_index("mp") // NZ, lax.axis_index("mp") % NZ
    runs, dxs, dzs = [], [], []
    for index, piece in enumerate(pieces):
        for offset, segment in enumerate(piece.segments):
            if segment is None:
                continue
            part, dx, dz, k = segment
            joins = (
                runs
                and runs[-1][0] == index
                and runs[-1][2] == part
                and (dxs[-1], dzs[-1]) == (dx, dz)
                and runs[-1][3] + runs[-1][4] == k
            )
            if joins:
                runs[-1] = (*runs[-1][:4], runs[-1][4] + 1)
            else:
                runs.append((index, offset, part, k, 1))
                dxs.append(dx)
                dzs.append(dz)
    rows = SEG * sum(run[4] for run in runs)
    blocks = (x - jnp.array(dxs, jnp.int32) + NX) % NX * NZ + (
        z - jnp.array(dzs, jnp.int32) + NZ
    ) % NZ
    vmem = pl.BlockSpec(memory_space=pltpu.VMEM)
    starts = [] if start is None else [start]
    return pl.pallas_call(
        functools.partial(low_kernel, len(pieces), runs, bool(starts), last),
        out_shape=[jax.ShapeDtypeStruct((NY, 2, R // NY // 2, 256), jnp.float32)] * 2
        if last
        else jax.ShapeDtypeStruct((2 * NY, 2, R // NY // 2, 256), jnp.float32),
        in_specs=[pl.BlockSpec(memory_space=pltpu.SMEM)]
        + [vmem] * (2 + len(pieces) + len(starts)),
        out_specs=[vmem] * 2 if last else vmem,
        compiler_params=pltpu.CompilerParams(vmem_limit_bytes=20 << 20),
        cost_estimate=pl.CostEstimate(
            flops=2 * rows * R * 256, bytes_accessed=rows * 1024, transcendentals=0
        ),
    )(jnp.append(blocks, core), *grads, *[p.array for p in pieces], *starts)


def spread_along_x(own):
    h = own.shape[0] // 2
    ahead, behind = shift(own, 1, 0), shift(own, -1, 0)
    ahead, behind, own = bar((ahead, behind, own))
    far = shift(ahead[:h], 1, 0), shift(behind[h:], -1, 0)
    own_other = other_core(own)
    near_other = other_core(ahead), other_core(behind)
    places = [(0, 0), (1, 0), (-1, 0), (2, 0), (2, h)]
    arrays = [own, ahead, behind, *far]
    others = [own_other, *near_other, *[other_core(f) for f in far]]
    return [(a, *p) for a, p in zip(arrays, places)], [(a, *p) for a, p in zip(others, places)]


def project_kernel(firsts, count, table, acts_in, grad_out, *refs):
    own, other, outs = refs[:count], refs[count : 2 * count], refs[2 * count : -2]
    held, arrived = refs[-2:]
    sizes = [part.shape[0] for part in own]
    copies = []
    for side, left in enumerate((acts_in, grad_out)):
        for k, size in enumerate(sizes):
            here = pl.multiple_of(table[1 + k] * (NZ * SEG) + firsts[k], SEG)
            copies.append(
                pltpu.make_async_copy(
                    left.at[:, pl.ds(here, size)],
                    held.at[side, :, pl.ds(sum(sizes[:k]), size)],
                    arrived.at[side, k],
                )
            )
            copies[-1].start()

    def run(*bases):
        for side, (parts, out) in enumerate(zip(bases, outs)):
            proj = None
            for k, part in enumerate(parts):
                copies[side * count + k].wait()
                at = sum(sizes[:k])
                product = jnp.dot(
                    held[side, :, at : at + sizes[k]], part[...], preferred_element_type=jnp.float32
                )
                proj = product if proj is None else proj + product
            proj = proj.T.astype(jnp.bfloat16)
            for j in range(PART):
                out[j] = proj[:, j * SEG : (j + 1) * SEG]

    both_ways(table[0], run, own, other)


def delta_kernel(firsts, count, table, steps, *refs):
    own, other = refs[:count], refs[count : 2 * count]
    delta_in, delta_out, held_in, held_out, left = refs[2 * count :]

    def run(parts_in, parts_out):
        copies = []

        def send(source, target, k):
            copies.append(pltpu.make_async_copy(source, target, left.at[len(copies)]))
            copies[-1].start()

        step = steps[:, 0].reshape(R, 256)
        for k, part in enumerate(parts_in):
            rows = part.shape[0]
            here = pl.ds(pl.multiple_of(table[1 + k] * (NZ * SEG) + firsts[k], SEG), rows)
            delta = jnp.dot(part[...], step, preferred_element_type=jnp.float32)
            held_in[here] = delta.astype(jnp.bfloat16)
            send(held_in.at[here], delta_in.at[here], k)
        step = steps[:, 1].reshape(R, 256).T
        for k, part in enumerate(parts_out):
            rows = part.shape[0]
            here = pl.ds(pl.multiple_of(table[1 + k] * (NZ * SEG) + firsts[k], SEG), rows)
            delta = lax.dot_general(
                step, part[...], (((1,), (1,)), ((), ())), preferred_element_type=jnp.float32
            )
            held_out[:, here] = delta.astype(jnp.bfloat16)
            send(held_out.at[:, here], delta_out.at[:, here], k)
        for copy in copies:
            copy.wait()

    both_ways(table[0], run, own, other)


def with_bases(kernel, out_shape, out_specs, scratch, flops, space, table, operands, own, other):
    vmem = pl.BlockSpec(memory_space=pltpu.VMEM)
    arrays = [a for a, _, _ in own + other]
    return pl.pallas_call(
        functools.partial(kernel, [first for _, _, first in own], len(own)),
        out_shape=out_shape,
        in_specs=[pl.BlockSpec(memory_space=pltpu.SMEM)]
        + [pl.BlockSpec(memory_space=space)] * len(operands)
        + [vmem] * len(arrays),
        out_specs=out_specs,
        scratch_shapes=scratch,
        compiler_params=pltpu.CompilerParams(vmem_limit_bytes=48 << 20),
        cost_estimate=pl.CostEstimate(flops=flops, bytes_accessed=8 << 20, transcendentals=0),
    )(table, *operands, *arrays)


def project(table, acts_in, grad_out, own, other):
    return with_bases(
        project_kernel,
        [jax.ShapeDtypeStruct((PART, R, SEG), jnp.bfloat16)] * 2,
        [pl.BlockSpec(memory_space=pltpu.VMEM)] * 2,
        [
            pltpu.VMEM((2, *acts_in.shape), jnp.bfloat16),
            pltpu.SemaphoreType.DMA((2, len(own))),
        ],
        4 * TOK * acts_in.shape[1] * R,
        pl.ANY,
        table,
        [acts_in, grad_out],
        own,
        other,
    )


def deltas(table, steps, own, other):
    width = NX * NZ * SEG
    shapes = [(width, 256), (256, width)]
    return with_bases(
        delta_kernel,
        [jax.ShapeDtypeStruct(shape, jnp.bfloat16) for shape in shapes],
        [pl.BlockSpec(memory_space=pl.ANY)] * 2,
        [pltpu.VMEM(shape, jnp.bfloat16) for shape in shapes]
        + [pltpu.SemaphoreType.DMA((2 * len(own),))],
        4 * 256 * width * R,
        pltpu.VMEM,
        table,
        [steps],
        own,
        other,
    )


def body(
    acts_in,
    grad_in,
    acts_out,
    grad_out,
    basis_in,
    basis_out,
    first_in,
    second_in,
    first_out,
    second_out,
):
    core = lax.axis_index("dp") % 2

    def mine(a, b):
        return jnp.where(core == 0, a, b)

    along_z = gather_direct(mine(basis_in, basis_out), "mp", GROUPS_Z)
    own, other = spread_along_x(along_z)
    x = lax.axis_index("mp") // NZ
    table = jnp.stack([core] + [(x - dx + NX) % NX for _, dx, _ in own])
    keep, give = gather_low(
        *project(table, acts_in, grad_out, own, other),
        functools.partial(low_of, (grad_in, acts_out), core),
    )
    shares = lax.all_to_all(
        keep + other_core(give), "dp", 0, 0, axis_index_groups=GROUPS_Y, tiled=True
    )
    share = (shares[0] + shares[1]) + (shares[2] + shares[3])
    new_first_in, new_second_in, step_in = adam_moments(share[0], first_in, second_in)
    new_first_out, new_second_out, step_out = adam_moments(share[1], first_out, second_out)
    steps = gather_direct(jnp.stack([step_in, step_out])[None], "dp")
    delta_in, delta_out = deltas(table, steps, own, other)
    return (
        delta_in,
        delta_out,
        new_first_in,
        new_second_in,
        new_first_out,
        new_second_out,
    )


def solution(mesh):
    in_specs = (
        P(("dp", "mp"), None),
        P("dp", "mp"),
        P("dp", "mp"),
        P(("dp", "mp"), None),
        P("mp", None),
        P("mp", None),
        P("dp", "mp"),
        P("dp", "mp"),
        P("dp", "mp"),
        P("dp", "mp"),
    )
    out_specs = (
        P(None, "mp"),
        P("mp", None),
        P("dp", "mp"),
        P("dp", "mp"),
        P("dp", "mp"),
        P("dp", "mp"),
    )
    return jax.shard_map(body, mesh=mesh, in_specs=in_specs, out_specs=out_specs, check_vma=False)
```

```python
import functools

import jax
import jax.numpy as jnp
from jax import lax
from jax.experimental import pallas as pl
from jax.experimental.pallas import tpu as pltpu
from jax.sharding import PartitionSpec as P

beta_one = 0.9
beta_two = 0.999
correct_one = 1.0 - 0.9**10
correct_two = 1.0 - 0.999**10
adam_eps = 1e-08

NX, NZ, NY = 4, 8, 4
TOK = 256
SEG = 128
PART = TOK // SEG
R = 256

GROUPS_Z = [[x * NZ + z for z in range(NZ)] for x in range(NX)]
GROUPS_Y = [[y * 2 + c for y in range(NY)] for c in range(2)]
GROUPS_X = [[x * NZ + z for x in range(NX)] for z in range(NZ)]

bar = lax.optimization_barrier


def adam_moments(low, first, second):
    new_first = beta_one * first + (1.0 - beta_one) * low
    new_second = beta_two * second + (1.0 - beta_two) * low * low
    direction = new_first / correct_one / (jnp.sqrt(new_second / correct_two) + adam_eps)
    return (new_first, new_second, direction.astype(jnp.bfloat16))


def shift(a, dx, dz):
    perm = [
        (x * NZ + z, (x + dx) % NX * NZ + (z + dz) % NZ) for x in range(NX) for z in range(NZ)
    ]
    return lax.ppermute(a, "mp", perm)


def other_core(a):
    return lax.ppermute(a, "dp", [(d, d ^ 1) for d in range(2 * NY)])


def gather_direct(a, axis, groups=None):
    n = len(groups[0]) if groups else lax.axis_size(axis)
    many = jnp.broadcast_to(a[None], (n, *a.shape))
    got = lax.all_to_all(many, axis, 0, 0, axis_index_groups=groups, tiled=True)
    return got.reshape(n * a.shape[0], *a.shape[1:])


class Piece:
    def __init__(self, array, segments):
        self.array, self.segments = array, segments

    def moved(self, dx, dz):
        return Piece(
            shift(self.array, dx, dz), [(p, x + dx, z + dz, k) for p, x, z, k in self.segments]
        )

    def cut(self, start, count):
        return Piece(self.array[start : start + count], self.segments[start : start + count])

    def halves(self):
        half = len(self.segments) // 2
        return self.cut(0, half), self.cut(half, half)


def pack_kernel(layout, *refs):
    count = 1 + max(source for packed in layout for source, _, _ in packed)
    for packed, out in zip(layout, refs[count:]):
        at = 0
        for source, start, segments in packed:
            out[at : at + segments] = refs[source][start : start + segments]
            at += segments


def pack(sources, layout):
    vmem = pl.BlockSpec(memory_space=pltpu.VMEM)
    sizes = [sum(run[2] for run in packed) for packed in layout]
    arrays = pl.pallas_call(
        functools.partial(pack_kernel, layout),
        out_shape=[jax.ShapeDtypeStruct((size, R, SEG), jnp.bfloat16) for size in sizes],
        in_specs=[vmem] * len(sources),
        out_specs=[vmem] * len(layout),
        compiler_params=pltpu.CompilerParams(vmem_limit_bytes=10 << 20),
    )(*[p.array for p in sources])
    return [
        Piece(array, [s for source, at, n in packed for s in sources[source].segments[at : at + n]])
        for array, packed in zip(arrays, layout)
    ]


def stack(pieces):
    return Piece(
        jnp.concatenate([p.array for p in pieces], 0), [s for p in pieces for s in p.segments]
    )


def together(*pieces):
    arrays = bar(tuple(p.array for p in pieces))
    return [Piece(a, p.segments) for a, p in zip(arrays, pieces)]


def with_low(pieces, low):
    *arrays, low = bar((*[p.array for p in pieces], low))
    return [Piece(a, p.segments) for a, p in zip(arrays, pieces)], low


def gather_low(proj_in, proj_out, add):
    n = PART
    a, b = (Piece(array, [(part, 0, 0, k) for k in range(n)]) for part, array in enumerate((proj_in, proj_out)))
    zp, zm, xp, xm = together(b.moved(0, 1), b.moved(0, -1), a.moved(1, 0), a.moved(-1, 0))
    zp2, zm2, x2a, x2b = together(
        zp.moved(0, 1), zm.moved(0, -1), xp.halves()[0].moved(1, 0), xm.halves()[1].moved(-1, 0)
    )
    h = n // 2
    four = [(0, 0, n), (1, 0, n), (2, 0, n), (3, 0, h), (4, 0, h)]
    up, down, side = pack(
        [a, xp, xm, x2a, x2b, b, zp, zm, zp2, zm2],
        [
            [(8, 0, n), *four],
            [(9, 0, n), *four],
            [(k, 0, n) for k in range(5, 10)],
        ],
    )
    sent = [Piece(up.array, [None] * n + up.segments[n:]), side]
    up, down, xp5, xm5 = together(
        up.moved(0, 1), down.moved(0, -1), side.moved(1, 0), side.moved(-1, 0)
    )
    low = add(sent, None)
    (up, down, xp5, xm5), low = with_low([up, down, xp5, xm5], low)
    s = pack(
        [up, down, xp5, xm5],
        [
            [(0, 0, h), (0, n, 4 * n)],
            [(1, h, h), (1, n, 4 * n)],
            [(2, 0, 5 * h), (0, 0, n), (1, 0, n)],
            [(3, 5 * h, 5 * h), (0, 0, n), (1, 0, n)],
        ],
    )
    u4, d4, p4, m4 = together(
        s[0].moved(0, 1), s[1].moved(0, -1), s[2].moved(1, 0), s[3].moved(-1, 0)
    )
    low = add([up, down, xp5, xm5], low)
    z4 = stack([u4.cut(0, h), d4.cut(0, h)])
    y3p, y3m = p4.cut(5 * h, 2 * n), m4.cut(5 * h, 2 * n)
    s, low = with_low(
        [
            u4.cut(h, 4 * n),
            d4.cut(h, 4 * n),
            stack([z4, y3p.halves()[0]]),
            stack([z4, y3m.halves()[1]]),
            z4,
        ],
        low,
    )
    u5, d5, p5, m5, q5 = together(
        s[0].moved(0, 1), s[1].moved(0, -1), s[2].moved(1, 0), s[3].moved(-1, 0), s[4].moved(2, 0)
    )
    low = add([u4, d4, p4, m4], low)
    s, low = with_low([u5.halves()[0], d5.halves()[1]], low)
    last = together(s[0].moved(0, 1), s[1].moved(0, -1))
    low = add([u5, d5, p5, m5, q5], low)
    return add(last, low, True)


def both_ways(core, run, own, other):
    @pl.when(core == 0)
    def _():
        run(own, other)

    @pl.when(core == 1)
    def _():
        run(other, own)


def low_kernel(count, runs, has_start, last, table, grad_in, acts_out, *refs):
    pieces, out_ref = refs[:count], refs[-2 if last else -1]
    totals = [refs[count][:, part].reshape(R, 256) if has_start else None for part in (0, 1)]
    for index, (piece, offset, part, first, segments) in enumerate(runs):
        left = [pieces[piece][offset + k] for k in range(segments)]
        left = jnp.concatenate(left, 1) if segments > 1 else left[0]
        row = pl.multiple_of(table[index] * TOK + first * SEG, SEG)
        right = (grad_in, acts_out)[part][pl.ds(row, segments * SEG)]
        product = jnp.dot(left, right, preferred_element_type=jnp.float32)
        totals[part] = product if totals[part] is None else totals[part] + product
    if not last:
        for part in (0, 1):
            out_ref[:, part] = totals[part].reshape(out_ref.shape[0], -1, 256)
        return

    def split(keep, give):
        for part in (0, 1):
            rows = totals[part].reshape(NY, 2, -1, 256)
            keep[:, part], give[:, part] = rows[:, 0], rows[:, 1]

    both_ways(table[len(runs)], split, refs[-2], refs[-1])


def low_of(grads, core, pieces, start, last=False):
    x, z = lax.axis_index("mp") // NZ, lax.axis_index("mp") % NZ
    runs, dxs, dzs = [], [], []
    for index, piece in enumerate(pieces):
        for offset, segment in enumerate(piece.segments):
            if segment is None:
                continue
            part, dx, dz, k = segment
            joins = (
                runs
                and runs[-1][0] == index
                and runs[-1][2] == part
                and (dxs[-1], dzs[-1]) == (dx, dz)
                and runs[-1][3] + runs[-1][4] == k
            )
            if joins:
                runs[-1] = (*runs[-1][:4], runs[-1][4] + 1)
            else:
                runs.append((index, offset, part, k, 1))
                dxs.append(dx)
                dzs.append(dz)
    rows = SEG * sum(run[4] for run in runs)
    blocks = (x - jnp.array(dxs, jnp.int32) + NX) % NX * NZ + (
        z - jnp.array(dzs, jnp.int32) + NZ
    ) % NZ
    vmem = pl.BlockSpec(memory_space=pltpu.VMEM)
    starts = [] if start is None else [start]
    return pl.pallas_call(
        functools.partial(low_kernel, len(pieces), runs, bool(starts), last),
        out_shape=[jax.ShapeDtypeStruct((NY, 2, R // NY // 2, 256), jnp.float32)] * 2
        if last
        else jax.ShapeDtypeStruct((2 * NY, 2, R // NY // 2, 256), jnp.float32),
        in_specs=[pl.BlockSpec(memory_space=pltpu.SMEM)]
        + [vmem] * (2 + len(pieces) + len(starts)),
        out_specs=[vmem] * 2 if last else vmem,
        compiler_params=pltpu.CompilerParams(vmem_limit_bytes=10 << 20),
        cost_estimate=pl.CostEstimate(
            flops=2 * rows * R * 256, bytes_accessed=rows * 1024, transcendentals=0
        ),
    )(jnp.append(blocks, core), *grads, *[p.array for p in pieces], *starts)


def spread_along_x(own):
    h = own.shape[0] // 2
    ahead, behind = shift(own, 1, 0), shift(own, -1, 0)
    ahead, behind, own = bar((ahead, behind, own))
    far = shift(ahead[:h], 1, 0), shift(behind[h:], -1, 0)
    own_other = other_core(own)
    near_other = other_core(ahead), other_core(behind)
    places = [(0, 0), (1, 0), (-1, 0), (2, 0), (2, h)]
    arrays = [own, ahead, behind, *far]
    others = [own_other, *near_other, *[other_core(f) for f in far]]
    return [(a, *p) for a, p in zip(arrays, places)], [(a, *p) for a, p in zip(others, places)]


def project_kernel(firsts, count, table, acts_in, grad_out, *refs):
    own, other, outs = refs[:count], refs[count : 2 * count], refs[2 * count : -2]
    held, arrived = refs[-2:]
    sizes = [part.shape[0] for part in own]
    copies = []
    for side, left in enumerate((acts_in, grad_out)):
        for k, size in enumerate(sizes):
            here = pl.multiple_of(table[1 + k] * (NZ * SEG) + firsts[k], SEG)
            copies.append(
                pltpu.make_async_copy(
                    left.at[:, pl.ds(here, size)],
                    held.at[side, :, pl.ds(sum(sizes[:k]), size)],
                    arrived.at[side, k],
                )
            )
            copies[-1].start()

    def run(*bases):
        for side, (parts, out) in enumerate(zip(bases, outs)):
            proj = None
            for k, part in enumerate(parts):
                copies[side * count + k].wait()
                at = sum(sizes[:k])
                product = jnp.dot(
                    held[side, :, at : at + sizes[k]], part[...], preferred_element_type=jnp.float32
                )
                proj = product if proj is None else proj + product
            proj = proj.T.astype(jnp.bfloat16)
            for j in range(PART):
                out[j] = proj[:, j * SEG : (j + 1) * SEG]

    both_ways(table[0], run, own, other)


def delta_kernel(firsts, count, table, steps, *refs):
    own, other = refs[:count], refs[count : 2 * count]
    delta_in, delta_out, held_in, held_out, left = refs[2 * count :]

    def run(parts_in, parts_out):
        copies = []

        def send(source, target, k):
            copies.append(pltpu.make_async_copy(source, target, left.at[len(copies)]))
            copies[-1].start()

        step = steps[:, 0].reshape(R, 256)
        for k, part in enumerate(parts_in):
            rows = part.shape[0]
            here = pl.ds(pl.multiple_of(table[1 + k] * (NZ * SEG) + firsts[k], SEG), rows)
            delta = jnp.dot(part[...], step, preferred_element_type=jnp.float32)
            held_in[here] = delta.astype(jnp.bfloat16)
            send(held_in.at[here], delta_in.at[here], k)
        step = steps[:, 1].reshape(R, 256).T
        for k, part in enumerate(parts_out):
            rows = part.shape[0]
            here = pl.ds(pl.multiple_of(table[1 + k] * (NZ * SEG) + firsts[k], SEG), rows)
            delta = lax.dot_general(
                step, part[...], (((1,), (1,)), ((), ())), preferred_element_type=jnp.float32
            )
            held_out[:, here] = delta.astype(jnp.bfloat16)
            send(held_out.at[:, here], delta_out.at[:, here], k)
        for copy in copies:
            copy.wait()

    both_ways(table[0], run, own, other)


def with_bases(kernel, out_shape, out_specs, scratch, flops, space, table, operands, own, other):
    vmem = pl.BlockSpec(memory_space=pltpu.VMEM)
    arrays = [a for a, _, _ in own + other]
    return pl.pallas_call(
        functools.partial(kernel, [first for _, _, first in own], len(own)),
        out_shape=out_shape,
        in_specs=[pl.BlockSpec(memory_space=pltpu.SMEM)]
        + [pl.BlockSpec(memory_space=space)] * len(operands)
        + [vmem] * len(arrays),
        out_specs=out_specs,
        scratch_shapes=scratch,
        compiler_params=pltpu.CompilerParams(vmem_limit_bytes=48 << 20),
        cost_estimate=pl.CostEstimate(flops=flops, bytes_accessed=8 << 20, transcendentals=0),
    )(table, *operands, *arrays)


def project(table, acts_in, grad_out, own, other):
    return with_bases(
        project_kernel,
        [jax.ShapeDtypeStruct((PART, R, SEG), jnp.bfloat16)] * 2,
        [pl.BlockSpec(memory_space=pltpu.VMEM)] * 2,
        [
            pltpu.VMEM((2, *acts_in.shape), jnp.bfloat16),
            pltpu.SemaphoreType.DMA((2, len(own))),
        ],
        4 * TOK * acts_in.shape[1] * R,
        pl.ANY,
        table,
        [acts_in, grad_out],
        own,
        other,
    )


def deltas(table, steps, own, other):
    width = NX * NZ * SEG
    shapes = [(width, 256), (256, width)]
    return with_bases(
        delta_kernel,
        [jax.ShapeDtypeStruct(shape, jnp.bfloat16) for shape in shapes],
        [pl.BlockSpec(memory_space=pl.ANY)] * 2,
        [pltpu.VMEM(shape, jnp.bfloat16) for shape in shapes]
        + [pltpu.SemaphoreType.DMA((2 * len(own),))],
        4 * 256 * width * R,
        pltpu.VMEM,
        table,
        [steps],
        own,
        other,
    )


def body(
    acts_in,
    grad_in,
    acts_out,
    grad_out,
    basis_in,
    basis_out,
    first_in,
    second_in,
    first_out,
    second_out,
):
    core = lax.axis_index("dp") % 2

    def mine(a, b):
        return jnp.where(core == 0, a, b)

    along_z = gather_direct(mine(basis_in, basis_out), "mp", GROUPS_Z)
    own, other = spread_along_x(along_z)
    x = lax.axis_index("mp") // NZ
    table = jnp.stack([core] + [(x - dx + NX) % NX for _, dx, _ in own])
    keep, give = gather_low(
        *project(table, acts_in, grad_out, own, other),
        functools.partial(low_of, (grad_in, acts_out), core),
    )
    shares = lax.all_to_all(
        keep + other_core(give), "dp", 0, 0, axis_index_groups=GROUPS_Y, tiled=True
    )
    share = (shares[0] + shares[1]) + (shares[2] + shares[3])
    new_first_in, new_second_in, step_in = adam_moments(share[0], first_in, second_in)
    new_first_out, new_second_out, step_out = adam_moments(share[1], first_out, second_out)
    steps = gather_direct(jnp.stack([step_in, step_out])[None], "dp")
    delta_in, delta_out = deltas(table, steps, own, other)
    return (
        delta_in,
        delta_out,
        new_first_in,
        new_second_in,
        new_first_out,
        new_second_out,
    )


def solution(mesh):
    in_specs = (
        P(("dp", "mp"), None),
        P("dp", "mp"),
        P("dp", "mp"),
        P(("dp", "mp"), None),
        P("mp", None),
        P("mp", None),
        P("dp", "mp"),
        P("dp", "mp"),
        P("dp", "mp"),
        P("dp", "mp"),
    )
    out_specs = (
        P(None, "mp"),
        P("mp", None),
        P("dp", "mp"),
        P("dp", "mp"),
        P("dp", "mp"),
        P("dp", "mp"),
    )
    return jax.shard_map(body, mesh=mesh, in_specs=in_specs, out_specs=out_specs, check_vma=False)
```
